32 devices in a mesh: rep: 2 (over y), dp: 2 (over core), tp: 8 (over z, x).
Axes of the slice: x: 2, y: 2, z: 4, core: 2. Of those that a mesh axis runs over, the one named last changes fastest.
Arguments:
- tokens: bfloat16 [16, 8192], P(('rep', 'dp')), parts along dimension 0, may hold values from -6 to 6
- gain: bfloat16 [8192], replicated, may hold values from 0.099609375 to 1.8984375
- query_matrix: bfloat16 [8192, 8192], P(None, 'tp'), may hold values from -0.0625 to 0.0625
- key_value_weight: bfloat16 [8192, 2048], P('tp'), may hold values from -0.0625 to 0.0625
- output_weight: bfloat16 [8192, 8192], P('tp'), may hold values from -0.5 to 0.5
- adapter_down_factors: bfloat16 [16, 48, 8192], P(('dp', 'tp')), may hold values from -0.0625 to 0.0625
- adapter_up_query: bfloat16 [16, 16, 8192], P(('dp', 'tp')), may hold values from -1.5 to 1.5
- adapter_up_key_value: bfloat16 [16, 2, 16, 1024], P(('dp', 'tp')), may hold values from -1.5 to 1.5
- tenant_slot_table: int32 [16], replicated, may hold values from 0 to 15, each once
- request_tenant_index: int32 [16], P('rep'), parts along dimension 0, may hold values from 0 to 15, as said below
- lengths: int32 [4, 4], P(('rep', 'dp')), parts along dimension 0, may hold values from 1 to 4096, 8192 in all within a row
- cache: bfloat16 [16, 32768, 256], P(('rep', 'dp'), 'tp'), parts along dimension 0, may hold values from -2000 to 2000
Outputs:
- mixed: bfloat16 [16, 8192], P(('rep', 'dp'), 'tp'), parts along dimension 0
The draws below stay inside these ranges and needn't reach their ends.
There are 2 independent parts, one for each index of `rep`. The reference program is written for one: setup_inputs(seed, part) draws one part's arguments, and reference() takes and returns one part's arrays. A program takes and returns all parts, laid end to end along the dimension named above; an argument that names none is the same for every part. Nothing has to cross between parts.
Inputs may be any that keep to these rules, and one draw needn't show every extreme that they name: `request_tenant_index`: in each subgroup of 4 requests one tenant is named by exactly 2 requests and every other tenant by at most one.
All inputs are finite; a program needn't handle non-finite values.
Results may differ from the reference program's by a relative error of at most 0.0095.
The reference program's roundings to bfloat16 on the way (of `normed`, `rank_vec` and `attended`) count: a program that leaves them out, or rounds other values in their place, can miss the bound.
Values may be sent and summed in bfloat16 or wider, within the bound.
A program may use at most 128 MiB of HBM per device.

```python
import math
import jax
import jax.numpy as jnp
import numpy as np
from jax import lax

MODEL_WIDTH = 8192
QUERY_HEADS = 64
KEY_VALUE_HEADS = 8
HEAD_SIZE = 128
ADAPTER_RANK = 16
REQS = 4
LEN = 4096
MOST = 2
REQS_ALL = 8
TENANT_COUNT = 16
N_DP = 2


def draw_request_tenant_index(key, part):
    key = jax.random.fold_in(key, 11)
    groups = REQS_ALL // REQS

    def one_group(group_key):
        hot_key, pick_key, place_key = jax.random.split(group_key, 3)
        hottest = jax.random.randint(hot_key, (), 0, TENANT_COUNT)
        others = (hottest + 1 + jax.random.permutation(pick_key, TENANT_COUNT - 1)[:REQS - MOST]) % TENANT_COUNT
        filled = jnp.concatenate([jnp.full((MOST,), hottest, jnp.int32), others.astype(jnp.int32)])
        placing = jax.random.permutation(place_key, REQS)
        return filled[placing]
    return jax.vmap(one_group)(jax.random.split(key, groups)).reshape(REQS_ALL).astype(jnp.int32)


def draw_cache(key, part):
    key = jax.random.fold_in(key, 23)
    base_key = jax.random.fold_in(key, 0)
    values = jnp.clip(jax.random.normal(base_key, (REQS_ALL, LEN * KEY_VALUE_HEADS, 2 * HEAD_SIZE), jnp.float32), -6.0, 6.0)
    return values.astype(jnp.bfloat16)


def block_scale(own_key, extent, pieces, smallest, high):
    def one(dim, blocks):
        heights = jax.random.uniform(jax.random.fold_in(jax.random.fold_in(own_key, 6), dim), (blocks,), jnp.float32, smallest / len(pieces), high / len(pieces))
        return jnp.repeat(jnp.exp(heights), extent[dim] // blocks).reshape((-1,) + (1,) * (len(extent) - dim - 1))

    level = one(*pieces[0])
    for cut in pieces[1:]:
        level = level * one(*cut)
    return level


def split_up(amount, total, limit, lean):
    weights = [(1 << 20) // math.isqrt(rank ** lean) + 1 for rank in range(2, amount + 1)]
    spare, counts = total - limit - (amount - 1), [1] * (amount - 1)
    while spare > 0:
        free = [i for i in range(amount - 1) if counts[i] < limit]
        pool, left = sum([weights[i] for i in free]), spare
        for i in free:
            addition = min(limit - counts[i], max(1, left * weights[i] // pool), spare)
            counts[i] = counts[i] + addition
            spare = spare - addition
    return np.array([limit] + counts)


def uneven_parts(key, amount, total, bound, slope):
    if amount == 2:
        one = jax.random.randint(key, (), max(1, total - bound), min(bound, total - 1) + 1)
        return jnp.stack([one, total - one])
    sizes = jnp.asarray(split_up(amount, total, bound, slope), jnp.int32)
    pairs = (amount - 1) // 2
    donor, receiver = sizes[1:1 + 2 * pairs:2], sizes[2:2 + 2 * pairs:2]
    margin = jnp.minimum(donor - 1, bound - receiver)
    passed = jax.random.randint(jax.random.fold_in(key, 1), (pairs,), 0, 1 << 20) % (margin + 1)
    sizes = sizes.at[1:1 + 2 * pairs:2].set(donor - passed).at[2:2 + 2 * pairs:2].set(receiver + passed)
    return sizes[jax.random.permutation(jax.random.fold_in(key, 2), amount)]


def scatter_about(stream_key, dims, width, limit, cuts=(), held_as=jnp.bfloat16):
    result = jax.random.normal(stream_key, dims, jnp.float32) * width
    if len(cuts) > 0:
        result = block_scale(stream_key, dims, cuts, -0.22, 0.18) * result
    return jnp.clip(result, min=-limit, max=limit).astype(held_as)


def setup_inputs(seed: int = 0, part: int = 0) -> dict:
    splits = jax.random.split(jax.random.key(seed), 13)
    own_keys = jax.random.split(jax.random.fold_in(splits[12], part), 13)
    tokens = scatter_about(own_keys[0], (REQS_ALL, MODEL_WIDTH), 1.0, 6.0, ((0, 2),))
    gain = jnp.clip(1.0 + 0.18 * jax.random.normal(splits[1], (MODEL_WIDTH,), jnp.float32), 0.099609375, 1.8984375).astype(jnp.bfloat16)
    query_matrix = scatter_about(splits[2], (MODEL_WIDTH, QUERY_HEADS * HEAD_SIZE), MODEL_WIDTH ** -0.5, 0.0625, ((1, 8),))
    key_value_weight = scatter_about(splits[3], (MODEL_WIDTH, 2 * KEY_VALUE_HEADS * HEAD_SIZE), MODEL_WIDTH ** -0.5, 0.0625, ((0, 8),))
    output_weight = scatter_about(splits[4], (QUERY_HEADS * HEAD_SIZE, MODEL_WIDTH), HEAD_SIZE ** -0.5, 0.5, ((0, 8),))
    adapter_down_factors = scatter_about(splits[5], (TENANT_COUNT, 3 * ADAPTER_RANK, MODEL_WIDTH), MODEL_WIDTH ** -0.5, 0.0625, ((0, 16),))
    adapter_up_query = scatter_about(splits[6], (TENANT_COUNT, ADAPTER_RANK, QUERY_HEADS * HEAD_SIZE), ADAPTER_RANK ** -0.5, 1.5, ((0, 16),))
    adapter_up_key_value = scatter_about(splits[7], (TENANT_COUNT, 2, ADAPTER_RANK, KEY_VALUE_HEADS * HEAD_SIZE), ADAPTER_RANK ** -0.5, 1.5, ((0, 16),))
    tenant_slot_table = jax.random.permutation(splits[8], TENANT_COUNT).astype(jnp.int32)
    request_tenant_index = draw_request_tenant_index(jax.random.fold_in(jax.random.fold_in(splits[12], part), 71), part)
    lengths = jax.vmap(lambda own: uneven_parts(own, REQS, REQS * LEN // 4 + LEN, LEN, 2))(jax.random.split(own_keys[10], N_DP)).reshape((N_DP, REQS)).astype(jnp.int32)
    cache = draw_cache(jax.random.fold_in(jax.random.fold_in(splits[12], part), 71), part)
    return dict(tokens=tokens, gain=gain, query_matrix=query_matrix, key_value_weight=key_value_weight, output_weight=output_weight, adapter_down_factors=adapter_down_factors, adapter_up_query=adapter_up_query, adapter_up_key_value=adapter_up_key_value, tenant_slot_table=tenant_slot_table, request_tenant_index=request_tenant_index, lengths=lengths, cache=cache)


theta_base = 500000.0
norm_eps = 1e-05

def rotate(vector, position):
    half_dim = vector.shape[-1] // 2
    frequency = jnp.power(jnp.float32(theta_base), -jnp.arange(half_dim, dtype=jnp.float32) * 2.0 / vector.shape[-1])
    angles = position.astype(jnp.float32)[..., None] * frequency
    cos_table = jnp.cos(angles)
    sin_table = jnp.sin(angles)
    leading = vector[..., :half_dim]
    trailing = vector[..., half_dim:]
    return jnp.concatenate([leading * cos_table - trailing * sin_table, trailing * cos_table + leading * sin_table], axis=-1)

def reference(tokens, gain, query_matrix, key_value_weight, output_weight, adapter_down_factors, adapter_up_query, adapter_up_key_value, tenant_slot_table, request_tenant_index, lengths, cache):
    widened = tokens.astype(jnp.float32)
    inverse_rms = lax.rsqrt(lax.optimization_barrier(jnp.mean(widened * widened, axis=1, keepdims=True)) + norm_eps)
    normed = (widened * inverse_rms * gain.astype(jnp.float32)).astype(jnp.bfloat16)
    request_slot_index = tenant_slot_table[request_tenant_index].astype(jnp.int32)
    chosen_down_factors = adapter_down_factors[request_slot_index]
    rank_vec = jnp.einsum('rd,rkd->rk', normed.astype(jnp.float32), chosen_down_factors.astype(jnp.float32)).astype(jnp.bfloat16)
    chosen_query_up = adapter_up_query[request_slot_index]
    query_raw = jnp.dot(normed, query_matrix, preferred_element_type=jnp.float32) + jnp.einsum('rk,rkc->rc', rank_vec[:, :ADAPTER_RANK].astype(jnp.float32), chosen_query_up.astype(jnp.float32))
    kv_base = jnp.dot(normed, key_value_weight, preferred_element_type=jnp.float32)
    chosen_key_value_up = adapter_up_key_value[request_slot_index]
    key_raw = kv_base[:, :KEY_VALUE_HEADS * HEAD_SIZE] + jnp.einsum('rk,rkc->rc', rank_vec[:, ADAPTER_RANK:2 * ADAPTER_RANK].astype(jnp.float32), chosen_key_value_up[:, 0].astype(jnp.float32))
    value_raw = kv_base[:, KEY_VALUE_HEADS * HEAD_SIZE:] + jnp.einsum('rk,rkc->rc', rank_vec[:, 2 * ADAPTER_RANK:].astype(jnp.float32), chosen_key_value_up[:, 1].astype(jnp.float32))
    positions = lengths.reshape(REQS_ALL).astype(jnp.int32)
    query = rotate(query_raw.reshape(REQS_ALL, QUERY_HEADS, HEAD_SIZE), positions[:, None]).astype(jnp.bfloat16)
    key_new = rotate(key_raw.reshape(REQS_ALL, KEY_VALUE_HEADS, HEAD_SIZE), positions[:, None]).astype(jnp.bfloat16)
    value_new = value_raw.reshape(REQS_ALL, KEY_VALUE_HEADS, HEAD_SIZE).astype(jnp.bfloat16)
    group_size = QUERY_HEADS // KEY_VALUE_HEADS
    factor = HEAD_SIZE ** (-0.5)

    def attend(request):
        query_row, key_row, value_row, length, cache_rows = request
        grouped = query_row.astype(jnp.float32).reshape(KEY_VALUE_HEADS, group_size, HEAD_SIZE)
        shaped = cache_rows.astype(jnp.float32).reshape(LEN, KEY_VALUE_HEADS, 2 * HEAD_SIZE).transpose(1, 0, 2)
        cached_keys = shaped[:, :, :HEAD_SIZE]
        cached_values = shaped[:, :, HEAD_SIZE:]
        scores = jnp.einsum('kgd,ktd->kgt', grouped, cached_keys) * factor
        usable = jnp.arange(LEN, dtype=jnp.int32) < length
        scores = jnp.where(usable[None, None, :], scores, -jnp.inf)
        own_score = jnp.einsum('kgd,kd->kg', grouped, key_row.astype(jnp.float32)) * factor
        highest = jnp.maximum(lax.optimization_barrier(jnp.max(scores, axis=2)), own_score)
        weights = jnp.exp(scores - highest[..., None])
        own_weight = jnp.exp(own_score - highest)
        totals = lax.optimization_barrier(jnp.sum(weights, axis=2)) + own_weight
        mixed_rows = jnp.einsum('kgt,ktd->kgd', weights, cached_values) + own_weight[..., None] * value_row.astype(jnp.float32)[:, None, :]
        return (mixed_rows / totals[..., None]).reshape(QUERY_HEADS * HEAD_SIZE).astype(jnp.bfloat16)
    attended = lax.map(attend, (query, key_new, value_new, positions, cache))
    return jnp.dot(attended, output_weight, preferred_element_type=jnp.float32).astype(jnp.bfloat16)
```

```python
import functools

import jax
import jax.numpy as jnp
import numpy as np
from jax import lax
from jax.experimental import pallas as pl
from jax.experimental.pallas import tpu as pltpu
from jax.sharding import PartitionSpec as P

QUERY_HEADS = 64
KEY_VALUE_HEADS = 8
HEAD_SIZE = 128
ADAPTER_RANK = 16


theta_base = 500000.0
norm_eps = 1e-05
neutral = -1e30


def combined_all(part, axis, combine):
    gathered = jax.tree.map(lambda a: lax.all_gather(a, axis), part)

    def take(source):
        return jax.tree.map(lambda a: lax.dynamic_index_in_dim(a, source, 0, False), gathered)

    return lax.fori_loop(
        1, lax.axis_size(axis), lambda source, state: combine(state, take(source)), take(0)
    )


def rotate(vector, position):
    half_dim = vector.shape[-1] // 2
    frequency = jnp.power(
        jnp.float32(theta_base), -jnp.arange(half_dim, dtype=jnp.float32) * 2.0 / vector.shape[-1]
    )
    angles = position.astype(jnp.float32)[..., None] * frequency
    cos_table = jnp.cos(angles)
    sin_table = jnp.sin(angles)
    leading = vector[..., :half_dim]
    trailing = vector[..., half_dim:]
    return jnp.concatenate(
        [leading * cos_table - trailing * sin_table, trailing * cos_table + leading * sin_table],
        axis=-1,
    )


def slot_lookup(ids, tenant_slot_table):
    table = jnp.arange(tenant_slot_table.shape[0], dtype=jnp.int32)
    return jnp.sum(jnp.where(ids[:, None] == table[None, :], tenant_slot_table[None, :], 0), axis=1)


def combine_parts(earlier, later):
    top_early, total_early, acc_early = earlier
    top_late, total_late, acc_late = later
    highest = jnp.maximum(top_early, top_late)
    factor_early = jnp.exp(top_early - highest)
    factor_late = jnp.exp(top_late - highest)
    return (
        highest,
        total_early * factor_early + total_late * factor_late,
        acc_early * factor_early[..., None] + acc_late * factor_late[..., None],
    )


def on_device(
    tokens,
    gain,
    query_matrix,
    key_value_weight,
    output_weight,
    adapter_down_factors,
    adapter_up_query,
    adapter_up_key_value,
    tenant_slot_table,
    request_tenant_index,
    lengths,
    cache,
):
    tp_size = lax.axis_size("tp")
    dp_size = lax.axis_size("dp")
    tp_index = lax.axis_index("tp")
    dp_index = lax.axis_index("dp")
    requests = tokens.shape[0]
    per_dev = key_value_weight.shape[0]
    head_cols = query_matrix.shape[1]
    heads_here = head_cols // HEAD_SIZE
    group_size = QUERY_HEADS // KEY_VALUE_HEADS
    kv_span = tp_size // KEY_VALUE_HEADS
    kv_head = tp_index // kv_span
    span_pos = cache.shape[1] // KEY_VALUE_HEADS
    factor = HEAD_SIZE ** (-0.5)
    widened = tokens.astype(jnp.float32)
    inverse_rms = lax.rsqrt(jnp.mean(widened * widened, axis=1, keepdims=True) + norm_eps)
    normed = (widened * inverse_rms * gain.astype(jnp.float32)).astype(jnp.bfloat16)
    own_cols = lax.dynamic_slice_in_dim(normed, tp_index * per_dev, per_dev, 1)
    kv_part = jnp.dot(own_cols, key_value_weight, preferred_element_type=jnp.float32)
    device = dp_index * tp_size + tp_index
    request_index = lax.all_gather(normed, "dp", axis=0, tiled=True)
    all_slots = slot_lookup(request_tenant_index, tenant_slot_table)
    full_rank = lax.dot_general(
        request_index,
        adapter_down_factors[0],
        (((1,), (1,)), ((), ())),
        preferred_element_type=jnp.float32,
    )
    slot_rank_rows = jnp.where((all_slots == device)[:, None], full_rank, 0.0).astype(jnp.bfloat16)
    query_update = jnp.dot(
        slot_rank_rows[:, :ADAPTER_RANK], adapter_up_query[0], preferred_element_type=jnp.float32
    )
    delta_k = jnp.dot(
        slot_rank_rows[:, ADAPTER_RANK : 2 * ADAPTER_RANK],
        adapter_up_key_value[0, 0],
        preferred_element_type=jnp.float32,
    )
    delta_v = jnp.dot(
        slot_rank_rows[:, 2 * ADAPTER_RANK :],
        adapter_up_key_value[0, 1],
        preferred_element_type=jnp.float32,
    )
    q_blocks = query_update.reshape(dp_size, requests, tp_size, head_cols).transpose(0, 2, 1, 3)
    k_blocks = jnp.repeat(
        delta_k.reshape(dp_size, requests, KEY_VALUE_HEADS, HEAD_SIZE), kv_span, axis=2
    ).transpose(0, 2, 1, 3)
    v_blocks = jnp.repeat(
        delta_v.reshape(dp_size, requests, KEY_VALUE_HEADS, HEAD_SIZE), kv_span, axis=2
    ).transpose(0, 2, 1, 3)
    term = jnp.concatenate([q_blocks, k_blocks, v_blocks], axis=3).reshape(
        dp_size * tp_size, requests, head_cols + 2 * HEAD_SIZE
    )
    received = lax.psum_scatter(term, ("dp", "tp"), scatter_dimension=0, tiled=True)[0]
    kv_sum = lax.psum(kv_part, "tp")
    query_delta = received[:, :head_cols]
    key_delta = received[:, head_cols : head_cols + HEAD_SIZE]
    value_delta = received[:, head_cols + HEAD_SIZE :]
    query_raw = jnp.dot(normed, query_matrix, preferred_element_type=jnp.float32) + query_delta
    key_base = lax.dynamic_slice_in_dim(kv_sum, kv_head * HEAD_SIZE, HEAD_SIZE, 1)
    value_base = lax.dynamic_slice_in_dim(
        kv_sum, KEY_VALUE_HEADS * HEAD_SIZE + kv_head * HEAD_SIZE, HEAD_SIZE, 1
    )
    key_raw = key_base + key_delta
    value_raw = value_base + value_delta
    positions = lengths[0]
    query = rotate(query_raw.reshape(requests, heads_here, HEAD_SIZE), positions[:, None]).astype(
        jnp.bfloat16
    )
    key_new = rotate(key_raw, positions).astype(jnp.bfloat16)
    value_new = value_raw.astype(jnp.bfloat16)
    all_queries = lax.all_gather(query.reshape(requests, head_cols), "tp", axis=1, tiled=True)
    grouped = all_queries.reshape(requests, KEY_VALUE_HEADS, group_size, HEAD_SIZE)
    local_rows = cache.reshape(requests, span_pos, KEY_VALUE_HEADS, 2 * HEAD_SIZE)
    cached_keys = local_rows[..., :HEAD_SIZE]
    cached_values = local_rows[..., HEAD_SIZE:]
    scores = (
        jnp.einsum("rkgd,rpkd->rkgp", grouped, cached_keys, preferred_element_type=jnp.float32)
        * factor
    )
    slot_positions = tp_index * span_pos + jnp.arange(span_pos, dtype=jnp.int32)
    usable = (slot_positions[None, :] < positions[:, None])[:, None, None, :]
    scores = jnp.where(usable, scores, neutral)
    local_top = jnp.max(scores, axis=3)
    weights = jnp.where(usable, jnp.exp(scores - local_top[..., None]), 0.0)
    local_total = jnp.sum(weights, axis=3)
    local_acc = jnp.einsum("rkgp,rpkd->rkgd", weights, cached_values.astype(jnp.float32))
    local_top = local_top.reshape(requests, QUERY_HEADS)
    local_total = local_total.reshape(requests, QUERY_HEADS)
    local_acc = local_acc.reshape(requests, QUERY_HEADS, HEAD_SIZE)
    merged_top, merged_total, merged_acc = combined_all(
        (local_top, local_total, local_acc), "tp", combine_parts
    )
    first_head = tp_index * heads_here
    merged_top = lax.dynamic_slice_in_dim(merged_top, first_head, heads_here, 1)
    merged_total = lax.dynamic_slice_in_dim(merged_total, first_head, heads_here, 1)
    merged_acc = lax.dynamic_slice_in_dim(merged_acc, first_head, heads_here, 1)
    own_score = (
        jnp.einsum("rhd,rd->rh", query, key_new, preferred_element_type=jnp.float32) * factor
    )
    highest = jnp.maximum(merged_top, own_score)
    old_factor = jnp.exp(merged_top - highest)
    new_factor = jnp.exp(own_score - highest)
    totals = merged_total * old_factor + new_factor
    combined = (
        merged_acc * old_factor[..., None]
        + new_factor[..., None] * value_new.astype(jnp.float32)[:, None, :]
    )
    attended = (combined / totals[..., None]).reshape(requests, head_cols).astype(jnp.bfloat16)
    shares = lax.psum_scatter(
        lax.dot_general(
            output_weight, attended, (((0,), (1,)), ((), ())), preferred_element_type=jnp.float32
        ),
        "tp",
        scatter_dimension=0,
        tiled=True,
    )
    return shares.T.astype(jnp.bfloat16)


MESH = pl.DeviceIdType.MESH


def attention_kernel(
    n,
    table_ref,
    tenant_ref,
    length_ref,
    tokens_ref,
    gain_ref,
    freq_ref,
    query_hbm,
    kv_hbm,
    output_hbm,
    down_hbm,
    up_query_hbm,
    up_kv_hbm,
    cache_hbm,
    out_ref,
    wq,
    wkv,
    wo,
    cache,
    down,
    up_query,
    up_kv,
    normed_chunks,
    cos_ref,
    sin_ref,
    rows_ref,
    value_ref,
    term_send,
    term_recv,
    all_queries,
    score_ref,
    part_send,
    part_recv,
    flat_ref,
    share_send,
    share_recv,
    wq_sem,
    kv_sem,
    wo_sem,
    cache_sem,
    own_sem,
    adapter_send,
    adapter_recv,
    send_sem,
    recv_sem,
):
    me = lax.axis_index("tp")
    core = lax.axis_index("dp")
    reqs = tokens_ref.shape[0]
    chunks = wq.shape[0]
    depth = wq.shape[1]
    cols = wq.shape[2]
    width = normed_chunks.shape[0] * normed_chunks.shape[2]
    span = cache.shape[1]
    heads = cols // HEAD_SIZE
    factor = HEAD_SIZE ** (-0.5)

    own_adapter = [
        pltpu.make_async_copy(down_hbm.at[0], down.at[0], own_sem.at[0]),
        pltpu.make_async_copy(up_query_hbm.at[0], up_query.at[0], own_sem.at[1]),
        pltpu.make_async_copy(up_kv_hbm.at[0], up_kv.at[0], own_sem.at[2]),
    ]
    kv_copy = pltpu.make_async_copy(kv_hbm, wkv, kv_sem)
    wq_copy = [
        pltpu.make_async_copy(query_hbm.at[pl.ds(c * depth, depth)], wq.at[c], wq_sem.at[c])
        for c in range(chunks)
    ]
    cache_copy = [
        pltpu.make_async_copy(cache_hbm.at[r], cache.at[r], cache_sem.at[r]) for r in range(reqs)
    ]
    wo_copy = [
        pltpu.make_async_copy(output_hbm.at[:, pl.ds(c * cols, cols)], wo.at[c], wo_sem.at[c])
        for c in range(n)
    ]

    def peer(k):
        return lax.rem(me + k, n)

    barrier = pltpu.get_barrier_semaphore()
    pl.semaphore_signal(barrier, inc=1, device_id={"dp": 1 - core}, device_id_type=MESH)
    for k in range(1, n):
        pl.semaphore_signal(barrier, inc=1, device_id={"tp": peer(k)}, device_id_type=MESH)
    for copy in own_adapter + [kv_copy] + wq_copy + cache_copy + wo_copy:
        copy.start()

    wide = tokens_ref[...].astype(jnp.float32)
    inverse = lax.rsqrt(jnp.sum(wide * wide, axis=1, keepdims=True) / width + norm_eps)
    normed = (wide * inverse * gain_ref[...].astype(jnp.float32)).astype(jnp.bfloat16)
    for c in range(chunks):
        normed_chunks[c] = normed[:, c * depth : (c + 1) * depth]

    table_rows = rows_ref.shape[0]
    row = lax.broadcasted_iota(jnp.int32, (table_rows, HEAD_SIZE), 0)
    lane_t = lax.broadcasted_iota(jnp.int32, (table_rows, HEAD_SIZE), 1)
    request = jnp.where(row < reqs * heads, row // heads, row - reqs * heads)
    place = jnp.zeros((table_rows, HEAD_SIZE), jnp.int32)
    for r in range(reqs):
        place = jnp.where(request == r, length_ref[0, r], place)
    angle = place.astype(jnp.float32) * freq_ref[...]
    cos_ref[...] = jnp.cos(angle)
    sin_ref[...] = jnp.where(lane_t < HEAD_SIZE // 2, -1.0, 1.0) * jnp.sin(angle)
    rows_ref[...] = jnp.zeros_like(rows_ref)

    pl.semaphore_wait(barrier, n)

    adapter = [
        pltpu.make_async_remote_copy(
            src_ref=source,
            dst_ref=target,
            send_sem=adapter_send.at[i],
            recv_sem=adapter_recv.at[i],
            device_id={"dp": 1 - core},
            device_id_type=MESH,
        )
        for i, (source, target) in enumerate(
            (
                (down_hbm.at[0], down.at[1]),
                (up_query_hbm.at[0], up_query.at[1]),
                (up_kv_hbm.at[0], up_kv.at[1]),
            )
        )
    ]
    for copy in adapter:
        copy.start()

    kv_copy.wait()
    kv_part = jnp.dot(normed_chunks[me], wkv[...], preferred_element_type=jnp.float32)
    for copy in own_adapter:
        copy.wait()
    for copy in adapter:
        copy.wait()
    which = lax.broadcasted_iota(jnp.int32, (reqs, 3 * ADAPTER_RANK), 0)
    slots = jnp.zeros((reqs, 3 * ADAPTER_RANK), jnp.int32)
    for r in range(reqs):
        slots = jnp.where(which == r, table_ref[tenant_ref[core * reqs + r]], slots)
    rank_rows = []
    for a in range(2):
        device = jnp.where(a == 0, core, 1 - core) * n + me
        full = lax.dot_general(
            normed, down[a], (((1,), (1,)), ((), ())), preferred_element_type=jnp.float32
        )
        rank_rows.append(jnp.where(slots == device, full, 0.0).astype(jnp.bfloat16))
    kv_terms = []
    for i in range(2):
        first = (i + 1) * ADAPTER_RANK
        term = kv_part[:, i * KEY_VALUE_HEADS * HEAD_SIZE : (i + 1) * KEY_VALUE_HEADS * HEAD_SIZE]
        for a in range(2):
            term = term + jnp.dot(
                rank_rows[a][:, first : first + ADAPTER_RANK],
                up_kv[a, i],
                preferred_element_type=jnp.float32,
            )
        kv_terms.append(term)
    for p in range(n):
        term = sum(
            jnp.dot(
                rank_rows[a][:, :ADAPTER_RANK],
                up_query[a, :, p * cols : (p + 1) * cols],
                preferred_element_type=jnp.float32,
            )
            for a in range(2)
        )
        term_send[p, :, :cols] = term
        for i in range(2):
            term_send[p, :, cols + i * HEAD_SIZE : cols + (i + 1) * HEAD_SIZE] = kv_terms[i][
                :, p * HEAD_SIZE : (p + 1) * HEAD_SIZE
            ]

    def sends(phase, source, target):
        return [
            pltpu.make_async_remote_copy(
                src_ref=source(k),
                dst_ref=target(k),
                send_sem=send_sem.at[phase, k],
                recv_sem=recv_sem.at[phase, k],
                device_id={"tp": peer(k)},
                device_id_type=MESH,
            )
            for k in range(1, n)
        ]

    term_copy = sends(0, lambda k: term_send.at[peer(k)], lambda k: term_recv.at[k])
    for copy in term_copy:
        copy.start()

    query_raw = jnp.zeros((reqs, cols), jnp.float32)
    for c in range(chunks):
        wq_copy[c].wait()
        query_raw = query_raw + jnp.dot(
            normed_chunks[c], wq[c], preferred_element_type=jnp.float32
        )
    for copy in term_copy:
        copy.wait_recv()
    received = term_send[me]
    for k in range(1, n):
        received = received + term_recv[k]
    query_raw = query_raw + received[:, :cols]
    for r in range(reqs):
        for h in range(heads):
            rows_ref[r * heads + h : r * heads + h + 1, :] = query_raw[
                r : r + 1, h * HEAD_SIZE : (h + 1) * HEAD_SIZE
            ]
    rows_ref[reqs * heads : reqs * heads + reqs, :] = received[:, cols : cols + HEAD_SIZE]
    value_ref[...] = received[:, cols + HEAD_SIZE :].astype(jnp.bfloat16).astype(jnp.float32)
    plain = rows_ref[...]
    rotated = plain * cos_ref[...] + pltpu.roll(plain, HEAD_SIZE // 2, 1) * sin_ref[...]
    rotated = rotated.astype(jnp.bfloat16)
    all_queries[me] = rotated[: reqs * heads]
    query_copy = sends(1, lambda k: all_queries.at[me], lambda k: all_queries.at[me])
    for copy in query_copy:
        copy.start()
    rounded = rotated.astype(jnp.float32)
    own_scores = []
    for r in range(reqs):
        key_row = rounded[reqs * heads + r : reqs * heads + r + 1]
        own_scores.append(
            jnp.sum(rounded[r * heads : (r + 1) * heads] * key_row, axis=1, keepdims=True) * factor
        )
    for copy in query_copy:
        copy.wait_recv()

    groups = KEY_VALUE_HEADS
    grouped = all_queries[...].astype(jnp.float32)
    piece = 512
    pieces = span // piece
    lane = lax.broadcasted_iota(jnp.int32, (heads, piece), 1)
    lane_tile = lax.broadcasted_iota(jnp.int32, (heads, HEAD_SIZE), 1)
    marks = jnp.zeros((heads, HEAD_SIZE), jnp.float32)
    for r in range(reqs):
        cache_copy[r].wait()
        limit = length_ref[0, r] - me * (span // groups)
        query_r = grouped[:, r * heads : (r + 1) * heads, :].reshape(n * heads, HEAD_SIZE)
        query_r = query_r.astype(jnp.bfloat16)
        top = jnp.full((heads, HEAD_SIZE), neutral, jnp.float32)
        for c in range(pieces):
            dots = lax.dot_general(
                query_r,
                cache[r, c * piece : (c + 1) * piece, :HEAD_SIZE],
                (((1,), (1,)), ((), ())),
                preferred_element_type=jnp.float32,
            )
            scores = dots[:heads]
            for g in range(1, groups):
                scores = jnp.where(
                    lane % groups == g, dots[g * heads : (g + 1) * heads], scores
                )
            usable = (lane + c * piece) // groups < limit
            scores = jnp.where(usable, scores * factor, neutral)
            score_ref[:, c * piece : (c + 1) * piece] = scores
            for i in range(piece // HEAD_SIZE):
                top = jnp.maximum(top, scores[:, i * HEAD_SIZE : (i + 1) * HEAD_SIZE])
        shift = groups
        while shift < HEAD_SIZE:
            top = jnp.maximum(top, pltpu.roll(top, shift, 1))
            shift *= 2
        top_wide = jnp.concatenate([top] * (piece // HEAD_SIZE), axis=1)
        total = jnp.zeros((heads, HEAD_SIZE), jnp.float32)
        acc = jnp.zeros((n * heads, HEAD_SIZE), jnp.float32)
        for c in range(pieces):
            usable = (lane + c * piece) // groups < limit
            weights = jnp.where(
                usable, jnp.exp(score_ref[:, c * piece : (c + 1) * piece] - top_wide), 0.0
            )
            for i in range(piece // HEAD_SIZE):
                total = total + weights[:, i * HEAD_SIZE : (i + 1) * HEAD_SIZE]
            spread = jnp.concatenate(
                [jnp.where(lane % groups == g, weights, 0.0) for g in range(groups)], axis=0
            ).astype(jnp.bfloat16)
            acc = acc + jnp.dot(
                spread,
                cache[r, c * piece : (c + 1) * piece, HEAD_SIZE:],
                preferred_element_type=jnp.float32,
            )
        shift = groups
        while shift < HEAD_SIZE:
            total = total + pltpu.roll(total, shift, 1)
            shift *= 2
        marks = jnp.where(lane_tile // groups == r, top, marks)
        marks = jnp.where(lane_tile // groups == reqs + r, total, marks)
        for g in range(groups):
            part_send[g, r] = acc[g * heads : (g + 1) * heads]
    for g in range(groups):
        part_send[g, reqs] = marks
    part_copy = sends(2, lambda k: part_send.at[peer(k)], lambda k: part_recv.at[k])
    for copy in part_copy:
        copy.start()
    part_recv[0] = part_send[me]
    for copy in part_copy:
        copy.wait_recv()

    tiles = [part_recv[k, reqs] for k in range(n)]
    highest = functools.reduce(jnp.maximum, tiles)
    scales = [jnp.exp(tile - highest) for tile in tiles]
    totals = sum(
        scale * pltpu.roll(tile, HEAD_SIZE - reqs * groups, 1)
        for scale, tile in zip(scales, tiles)
    )
    for r in range(reqs):
        chosen = lane_tile == r * groups + me

        def pick(tile):
            return jnp.sum(jnp.where(chosen, tile, 0.0), axis=1, keepdims=True)

        merged = sum(pick(scales[k]) * part_recv[k, r] for k in range(n))
        merged_top = pick(highest)
        top_all = jnp.maximum(merged_top, own_scores[r])
        old = jnp.exp(merged_top - top_all)
        new = jnp.exp(own_scores[r] - top_all)
        attended = (merged * old + new * value_ref[r : r + 1, :]) / (pick(totals) * old + new)
        for h in range(heads):
            flat_ref[r : r + 1, h * HEAD_SIZE : (h + 1) * HEAD_SIZE] = attended[h : h + 1]
    attended = flat_ref[...].astype(jnp.bfloat16)

    for copy in wo_copy:
        copy.wait()
    share_copy = sends(3, lambda k: share_send.at[peer(k)], lambda k: share_recv.at[k])
    for k in range(1, n):
        share_send[peer(k)] = jnp.dot(
            attended, wo[peer(k)], preferred_element_type=jnp.float32
        )
        share_copy[k - 1].start()
    mixed = jnp.dot(attended, wo[me], preferred_element_type=jnp.float32)
    for k in range(1, n):
        share_copy[k - 1].wait_recv()
        mixed = mixed + share_recv[k]
    out_ref[...] = mixed
    for copy in term_copy + query_copy + part_copy + share_copy:
        copy.wait_send()


def on_device_fused(
    tokens,
    gain,
    query_matrix,
    key_value_weight,
    output_weight,
    adapter_down_factors,
    adapter_up_query,
    adapter_up_key_value,
    tenant_slot_table,
    request_tenant_index,
    lengths,
    cache,
):
    n = lax.axis_size("tp")
    reqs, width = tokens.shape
    cols = query_matrix.shape[1]
    heads = cols // HEAD_SIZE
    rows = -(-(reqs * heads + reqs) // 8) * 8
    half = HEAD_SIZE // 2
    power = np.arange(HEAD_SIZE) % half * 2.0 / HEAD_SIZE
    frequency = jnp.asarray((theta_base ** -power).astype(np.float32)[None, :])
    smem = pl.BlockSpec(memory_space=pltpu.SMEM)
    vmem = pl.BlockSpec(memory_space=pltpu.VMEM)
    hbm = pl.BlockSpec(memory_space=pl.ANY)
    bf16, f32 = jnp.bfloat16, jnp.float32
    dma = pltpu.SemaphoreType.DMA
    share = pl.pallas_call(
        functools.partial(attention_kernel, n),
        out_shape=jax.ShapeDtypeStruct((reqs, cols), f32),
        in_specs=[smem] * 3 + [vmem] * 3 + [hbm] * 7,
        out_specs=vmem,
        scratch_shapes=[
            pltpu.VMEM((n, width // n, cols), bf16),
            pltpu.VMEM(key_value_weight.shape, bf16),
            pltpu.VMEM((n, output_weight.shape[0], width // n), bf16),
            pltpu.VMEM(cache.shape, bf16),
            pltpu.VMEM((2,) + adapter_down_factors.shape[1:], bf16),
            pltpu.VMEM((2,) + adapter_up_query.shape[1:], bf16),
            pltpu.VMEM((2,) + adapter_up_key_value.shape[1:], bf16),
            pltpu.VMEM((n, reqs, width // n), bf16),
            pltpu.VMEM((rows, HEAD_SIZE), f32),
            pltpu.VMEM((rows, HEAD_SIZE), f32),
            pltpu.VMEM((rows, HEAD_SIZE), f32),
            pltpu.VMEM((reqs, HEAD_SIZE), f32),
            pltpu.VMEM((n, reqs, cols + 2 * HEAD_SIZE), f32),
            pltpu.VMEM((n, reqs, cols + 2 * HEAD_SIZE), f32),
            pltpu.VMEM((n, reqs * heads, HEAD_SIZE), bf16),
            pltpu.VMEM((heads, cache.shape[1]), f32),
            pltpu.VMEM((n, reqs + 1, heads, HEAD_SIZE), f32),
            pltpu.VMEM((n, reqs + 1, heads, HEAD_SIZE), f32),
            pltpu.VMEM((reqs, cols), f32),
            pltpu.VMEM((n, reqs, width // n), f32),
            pltpu.VMEM((n, reqs, width // n), f32),
            dma((n,)),
            dma,
            dma((n,)),
            dma((reqs,)),
            dma((3,)),
            dma((3,)),
            dma((3,)),
            dma((4, n)),
            dma((4, n)),
        ],
        compiler_params=pltpu.CompilerParams(
            collective_id=0, has_side_effects=True, vmem_limit_bytes=60 * 2**20
        ),
    )(
        tenant_slot_table,
        request_tenant_index,
        lengths,
        tokens,
        gain.reshape(1, width),
        frequency,
        query_matrix,
        key_value_weight,
        output_weight,
        adapter_down_factors,
        adapter_up_query,
        adapter_up_key_value,
        cache,
    )
    return share.astype(bf16)


def solution(mesh):
    in_specs = (
        P(("rep", "dp"), None),
        P(),
        P(None, "tp"),
        P("tp", None),
        P("tp", None),
        P(("dp", "tp"), None, None),
        P(("dp", "tp"), None, None),
        P(("dp", "tp"), None, None, None),
        P(),
        P("rep"),
        P(("rep", "dp"), None),
        P(("rep", "dp"), "tp", None),
    )
    out_specs = P(("rep", "dp"), "tp")
    fused = mesh.shape["tp"] == KEY_VALUE_HEADS and mesh.shape["dp"] == 2
    body = on_device_fused if fused else on_device
    return jax.shard_map(
        body, mesh=mesh, in_specs=in_specs, out_specs=out_specs, check_vma=False
    )
```

```python
import functools

import jax
import jax.numpy as jnp
import numpy as np
from jax import lax
from jax.experimental import pallas as pl
from jax.experimental.pallas import tpu as pltpu
from jax.sharding import PartitionSpec as P

QUERY_HEADS = 64
KEY_VALUE_HEADS = 8
HEAD_SIZE = 128
ADAPTER_RANK = 16


theta_base = 500000.0
norm_eps = 1e-05
neutral = -1e30


def combined_all(part, axis, combine):
    gathered = jax.tree.map(lambda a: lax.all_gather(a, axis), part)

    def take(source):
        return jax.tree.map(lambda a: lax.dynamic_index_in_dim(a, source, 0, False), gathered)

    return lax.fori_loop(
        1, lax.axis_size(axis), lambda source, state: combine(state, take(source)), take(0)
    )


def rotate(vector, position):
    half_dim = vector.shape[-1] // 2
    frequency = jnp.power(
        jnp.float32(theta_base), -jnp.arange(half_dim, dtype=jnp.float32) * 2.0 / vector.shape[-1]
    )
    angles = position.astype(jnp.float32)[..., None] * frequency
    cos_table = jnp.cos(angles)
    sin_table = jnp.sin(angles)
    leading = vector[..., :half_dim]
    trailing = vector[..., half_dim:]
    return jnp.concatenate(
        [leading * cos_table - trailing * sin_table, trailing * cos_table + leading * sin_table],
        axis=-1,
    )


def slot_lookup(ids, tenant_slot_table):
    table = jnp.arange(tenant_slot_table.shape[0], dtype=jnp.int32)
    return jnp.sum(jnp.where(ids[:, None] == table[None, :], tenant_slot_table[None, :], 0), axis=1)


def combine_parts(earlier, later):
    top_early, total_early, acc_early = earlier
    top_late, total_late, acc_late = later
    highest = jnp.maximum(top_early, top_late)
    factor_early = jnp.exp(top_early - highest)
    factor_late = jnp.exp(top_late - highest)
    return (
        highest,
        total_early * factor_early + total_late * factor_late,
        acc_early * factor_early[..., None] + acc_late * factor_late[..., None],
    )


def on_device(
    tokens,
    gain,
    query_matrix,
    key_value_weight,
    output_weight,
    adapter_down_factors,
    adapter_up_query,
    adapter_up_key_value,
    tenant_slot_table,
    request_tenant_index,
    lengths,
    cache,
):
    tp_size = lax.axis_size("tp")
    dp_size = lax.axis_size("dp")
    tp_index = lax.axis_index("tp")
    dp_index = lax.axis_index("dp")
    requests = tokens.shape[0]
    per_dev = key_value_weight.shape[0]
    head_cols = query_matrix.shape[1]
    heads_here = head_cols // HEAD_SIZE
    group_size = QUERY_HEADS // KEY_VALUE_HEADS
    kv_span = tp_size // KEY_VALUE_HEADS
    kv_head = tp_index // kv_span
    span_pos = cache.shape[1] // KEY_VALUE_HEADS
    factor = HEAD_SIZE ** (-0.5)
    widened = tokens.astype(jnp.float32)
    inverse_rms = lax.rsqrt(jnp.mean(widened * widened, axis=1, keepdims=True) + norm_eps)
    normed = (widened * inverse_rms * gain.astype(jnp.float32)).astype(jnp.bfloat16)
    own_cols = lax.dynamic_slice_in_dim(normed, tp_index * per_dev, per_dev, 1)
    kv_part = jnp.dot(own_cols, key_value_weight, preferred_element_type=jnp.float32)
    device = dp_index * tp_size + tp_index
    request_index = lax.all_gather(normed, "dp", axis=0, tiled=True)
    all_slots = slot_lookup(request_tenant_index, tenant_slot_table)
    full_rank = lax.dot_general(
        request_index,
        adapter_down_factors[0],
        (((1,), (1,)), ((), ())),
        preferred_element_type=jnp.float32,
    )
    slot_rank_rows = jnp.where((all_slots == device)[:, None], full_rank, 0.0).astype(jnp.bfloat16)
    query_update = jnp.dot(
        slot_rank_rows[:, :ADAPTER_RANK], adapter_up_query[0], preferred_element_type=jnp.float32
    )
    delta_k = jnp.dot(
        slot_rank_rows[:, ADAPTER_RANK : 2 * ADAPTER_RANK],
        adapter_up_key_value[0, 0],
        preferred_element_type=jnp.float32,
    )
    delta_v = jnp.dot(
        slot_rank_rows[:, 2 * ADAPTER_RANK :],
        adapter_up_key_value[0, 1],
        preferred_element_type=jnp.float32,
    )
    q_blocks = query_update.reshape(dp_size, requests, tp_size, head_cols).transpose(0, 2, 1, 3)
    k_blocks = jnp.repeat(
        delta_k.reshape(dp_size, requests, KEY_VALUE_HEADS, HEAD_SIZE), kv_span, axis=2
    ).transpose(0, 2, 1, 3)
    v_blocks = jnp.repeat(
        delta_v.reshape(dp_size, requests, KEY_VALUE_HEADS, HEAD_SIZE), kv_span, axis=2
    ).transpose(0, 2, 1, 3)
    term = jnp.concatenate([q_blocks, k_blocks, v_blocks], axis=3).reshape(
        dp_size * tp_size, requests, head_cols + 2 * HEAD_SIZE
    )
    received = lax.psum_scatter(term, ("dp", "tp"), scatter_dimension=0, tiled=True)[0]
    kv_sum = lax.psum(kv_part, "tp")
    query_delta = received[:, :head_cols]
    key_delta = received[:, head_cols : head_cols + HEAD_SIZE]
    value_delta = received[:, head_cols + HEAD_SIZE :]
    query_raw = jnp.dot(normed, query_matrix, preferred_element_type=jnp.float32) + query_delta
    key_base = lax.dynamic_slice_in_dim(kv_sum, kv_head * HEAD_SIZE, HEAD_SIZE, 1)
    value_base = lax.dynamic_slice_in_dim(
        kv_sum, KEY_VALUE_HEADS * HEAD_SIZE + kv_head * HEAD_SIZE, HEAD_SIZE, 1
    )
    key_raw = key_base + key_delta
    value_raw = value_base + value_delta
    positions = lengths[0]
    query = rotate(query_raw.reshape(requests, heads_here, HEAD_SIZE), positions[:, None]).astype(
        jnp.bfloat16
    )
    key_new = rotate(key_raw, positions).astype(jnp.bfloat16)
    value_new = value_raw.astype(jnp.bfloat16)
    all_queries = lax.all_gather(query.reshape(requests, head_cols), "tp", axis=1, tiled=True)
    grouped = all_queries.reshape(requests, KEY_VALUE_HEADS, group_size, HEAD_SIZE)
    local_rows = cache.reshape(requests, span_pos, KEY_VALUE_HEADS, 2 * HEAD_SIZE)
    cached_keys = local_rows[..., :HEAD_SIZE]
    cached_values = local_rows[..., HEAD_SIZE:]
    scores = (
        jnp.einsum("rkgd,rpkd->rkgp", grouped, cached_keys, preferred_element_type=jnp.float32)
        * factor
    )
    slot_positions = tp_index * span_pos + jnp.arange(span_pos, dtype=jnp.int32)
    usable = (slot_positions[None, :] < positions[:, None])[:, None, None, :]
    scores = jnp.where(usable, scores, neutral)
    local_top = jnp.max(scores, axis=3)
    weights = jnp.where(usable, jnp.exp(scores - local_top[..., None]), 0.0)
    local_total = jnp.sum(weights, axis=3)
    local_acc = jnp.einsum("rkgp,rpkd->rkgd", weights, cached_values.astype(jnp.float32))
    local_top = local_top.reshape(requests, QUERY_HEADS)
    local_total = local_total.reshape(requests, QUERY_HEADS)
    local_acc = local_acc.reshape(requests, QUERY_HEADS, HEAD_SIZE)
    merged_top, merged_total, merged_acc = combined_all(
        (local_top, local_total, local_acc), "tp", combine_parts
    )
    first_head = tp_index * heads_here
    merged_top = lax.dynamic_slice_in_dim(merged_top, first_head, heads_here, 1)
    merged_total = lax.dynamic_slice_in_dim(merged_total, first_head, heads_here, 1)
    merged_acc = lax.dynamic_slice_in_dim(merged_acc, first_head, heads_here, 1)
    own_score = (
        jnp.einsum("rhd,rd->rh", query, key_new, preferred_element_type=jnp.float32) * factor
    )
    highest = jnp.maximum(merged_top, own_score)
    old_factor = jnp.exp(merged_top - highest)
    new_factor = jnp.exp(own_score - highest)
    totals = merged_total * old_factor + new_factor
    combined = (
        merged_acc * old_factor[..., None]
        + new_factor[..., None] * value_new.astype(jnp.float32)[:, None, :]
    )
    attended = (combined / totals[..., None]).reshape(requests, head_cols).astype(jnp.bfloat16)
    shares = lax.psum_scatter(
        lax.dot_general(
            output_weight, attended, (((0,), (1,)), ((), ())), preferred_element_type=jnp.float32
        ),
        "tp",
        scatter_dimension=0,
        tiled=True,
    )
    return shares.T.astype(jnp.bfloat16)


MESH = pl.DeviceIdType.MESH


def attention_kernel(
    n,
    table_ref,
    tenant_ref,
    length_ref,
    tokens_ref,
    gain_ref,
    freq_ref,
    query_hbm,
    kv_hbm,
    output_hbm,
    down_hbm,
    up_query_hbm,
    up_kv_hbm,
    cache_hbm,
    out_ref,
    wq,
    wkv,
    wo,
    cache,
    down,
    up_query,
    up_kv,
    normed_chunks,
    cos_ref,
    sin_ref,
    rows_ref,
    value_ref,
    term_send,
    term_recv,
    all_queries,
    score_ref,
    part_send,
    part_recv,
    flat_ref,
    share_send,
    share_recv,
    wq_sem,
    kv_sem,
    wo_sem,
    cache_sem,
    own_sem,
    adapter_send,
    adapter_recv,
    send_sem,
    recv_sem,
):
    me = lax.axis_index("tp")
    core = lax.axis_index("dp")
    reqs = tokens_ref.shape[0]
    chunks = wq.shape[0]
    depth = wq.shape[1]
    cols = wq.shape[2]
    width = normed_chunks.shape[0] * normed_chunks.shape[2]
    span = cache.shape[1]
    heads = cols // HEAD_SIZE
    factor = HEAD_SIZE ** (-0.5)
    ranks = 3 * ADAPTER_RANK

    own_adapter = [
        pltpu.make_async_copy(down_hbm.at[0], down.at[pl.ds(0, ranks)], own_sem.at[0]),
        pltpu.make_async_copy(up_query_hbm.at[0], up_query.at[pl.ds(0, ADAPTER_RANK)], own_sem.at[1]),
        pltpu.make_async_copy(up_kv_hbm.at[0], up_kv.at[:, pl.ds(0, ADAPTER_RANK)], own_sem.at[2]),
    ]
    kv_copy = pltpu.make_async_copy(kv_hbm, wkv, kv_sem)
    wq_copy = [
        pltpu.make_async_copy(query_hbm.at[pl.ds(c * depth, depth)], wq.at[c], wq_sem.at[c])
        for c in range(chunks)
    ]
    cache_copy = [
        pltpu.make_async_copy(cache_hbm.at[r], cache.at[r], cache_sem.at[r]) for r in range(reqs)
    ]
    wo_copy = [
        pltpu.make_async_copy(output_hbm.at[:, pl.ds(c * cols, cols)], wo.at[c], wo_sem.at[c])
        for c in range(n)
    ]

    def peer(k):
        return lax.rem(me + k, n)

    barrier = pltpu.get_barrier_semaphore()
    pl.semaphore_signal(barrier, inc=1, device_id={"dp": 1 - core}, device_id_type=MESH)
    for k in range(1, n):
        pl.semaphore_signal(barrier, inc=1, device_id={"tp": peer(k)}, device_id_type=MESH)
    for copy in own_adapter + [kv_copy] + wq_copy:
        copy.start()

    wide = tokens_ref[...].astype(jnp.float32)
    inverse = lax.rsqrt(jnp.sum(wide * wide, axis=1, keepdims=True) / width + norm_eps)
    normed = (wide * inverse * gain_ref[...].astype(jnp.float32).reshape(1, width)).astype(jnp.bfloat16)
    for c in range(chunks):
        normed_chunks[c] = normed[:, c * depth : (c + 1) * depth]

    table_rows = rows_ref.shape[0]
    row = lax.broadcasted_iota(jnp.int32, (table_rows, HEAD_SIZE), 0)
    lane_t = lax.broadcasted_iota(jnp.int32, (table_rows, HEAD_SIZE), 1)
    request = jnp.where(row < reqs * heads, row // heads, row - reqs * heads)
    place = jnp.zeros((table_rows, HEAD_SIZE), jnp.int32)
    for r in range(reqs):
        place = jnp.where(request == r, length_ref[0, r], place)
    angle = place.astype(jnp.float32) * freq_ref[...]
    cos_ref[...] = jnp.cos(angle)
    sin_ref[...] = jnp.where(lane_t < HEAD_SIZE // 2, -1.0, 1.0) * jnp.sin(angle)
    rows_ref[...] = jnp.zeros_like(rows_ref)

    pl.semaphore_wait(barrier, n)

    adapter = [
        pltpu.make_async_remote_copy(
            src_ref=source,
            dst_ref=target,
            send_sem=adapter_send.at[i],
            recv_sem=adapter_recv.at[i],
            device_id={"dp": 1 - core},
            device_id_type=MESH,
        )
        for i, (source, target) in enumerate(
            (
                (down_hbm.at[0], down.at[pl.ds(ranks, ranks)]),
                (up_query_hbm.at[0], up_query.at[pl.ds(ADAPTER_RANK, ADAPTER_RANK)]),
                (up_kv_hbm.at[0], up_kv.at[:, pl.ds(ADAPTER_RANK, ADAPTER_RANK)]),
            )
        )
    ]
    for copy in adapter:
        copy.start()

    kv_copy.wait()
    for copy in cache_copy:
        copy.start()
    kv_part = jnp.dot(normed_chunks[me], wkv[...], preferred_element_type=jnp.float32)
    for copy in own_adapter:
        copy.wait()
    for copy in adapter:
        copy.wait()
    which = lax.broadcasted_iota(jnp.int32, (reqs, 2 * ranks), 0)
    slots = jnp.zeros((reqs, 2 * ranks), jnp.int32)
    for r in range(reqs):
        slots = jnp.where(which == r, table_ref[tenant_ref[core * reqs + r]], slots)
    owned = lax.broadcasted_iota(jnp.int32, (reqs, 2 * ranks), 1) < ranks
    device = jnp.where(owned, core, 1 - core) * n + me
    full = lax.dot_general(
        normed, down[...], (((1,), (1,)), ((), ())), preferred_element_type=jnp.float32
    )
    rank_rows = jnp.where(slots == device, full, 0.0)

    def rank_part(i):
        first = i * ADAPTER_RANK
        return jnp.concatenate(
            [
                rank_rows[:, first : first + ADAPTER_RANK],
                rank_rows[:, ranks + first : ranks + first + ADAPTER_RANK],
            ],
            axis=1,
        ).astype(jnp.bfloat16)

    kv_terms = []
    for i in range(2):
        kv_terms.append(
            kv_part[:, i * KEY_VALUE_HEADS * HEAD_SIZE : (i + 1) * KEY_VALUE_HEADS * HEAD_SIZE]
            + jnp.dot(rank_part(i + 1), up_kv[i], preferred_element_type=jnp.float32)
        )
    query_rank = rank_part(0)
    for p in range(n):
        term_send[p, :, :cols] = jnp.dot(
            query_rank, up_query[:, p * cols : (p + 1) * cols], preferred_element_type=jnp.float32
        )
        for i in range(2):
            term_send[p, :, cols + i * HEAD_SIZE : cols + (i + 1) * HEAD_SIZE] = kv_terms[i][
                :, p * HEAD_SIZE : (p + 1) * HEAD_SIZE
            ]

    def sends(phase, source, target):
        return [
            pltpu.make_async_remote_copy(
                src_ref=source(k),
                dst_ref=target(k),
                send_sem=send_sem.at[phase, k],
                recv_sem=recv_sem.at[phase, k],
                device_id={"tp": peer(k)},
                device_id_type=MESH,
            )
            for k in range(1, n)
        ]

    term_copy = sends(0, lambda k: term_send.at[peer(k)], lambda k: term_recv.at[k])
    for copy in term_copy:
        copy.start()
    for copy in wo_copy:
        copy.start()

    query_raw = jnp.zeros((reqs, cols), jnp.float32)
    for c in range(chunks):
        wq_copy[c].wait()
        query_raw = query_raw + jnp.dot(
            normed_chunks[c], wq[c], preferred_element_type=jnp.float32
        )
    for copy in term_copy:
        copy.wait_recv()
    received = term_send[me]
    for k in range(1, n):
        received = received + term_recv[k]
    query_raw = query_raw + received[:, :cols]
    for r in range(reqs):
        for h in range(heads):
            rows_ref[r * heads + h : r * heads + h + 1, :] = query_raw[
                r : r + 1, h * HEAD_SIZE : (h + 1) * HEAD_SIZE
            ]
    rows_ref[reqs * heads : reqs * heads + reqs, :] = received[:, cols : cols + HEAD_SIZE]
    value_ref[...] = received[:, cols + HEAD_SIZE :].astype(jnp.bfloat16).astype(jnp.float32)
    plain = rows_ref[...]
    rotated = plain * cos_ref[...] + pltpu.roll(plain, HEAD_SIZE // 2, 1) * sin_ref[...]
    rotated = rotated.astype(jnp.bfloat16)
    all_queries[me] = rotated[: reqs * heads]
    query_copy = sends(1, lambda k: all_queries.at[me], lambda k: all_queries.at[me])
    for copy in query_copy:
        copy.start()
    rounded = rotated.astype(jnp.float32)
    own_scores = []
    for r in range(reqs):
        key_row = rounded[reqs * heads + r : reqs * heads + r + 1]
        own_scores.append(
            jnp.sum(rounded[r * heads : (r + 1) * heads] * key_row, axis=1, keepdims=True) * factor
        )
    for copy in query_copy:
        copy.wait_recv()

    groups = KEY_VALUE_HEADS
    grouped = all_queries[...].astype(jnp.float32)
    piece = 512
    pieces = span // piece
    lane = lax.broadcasted_iota(jnp.int32, (heads, piece), 1)
    lane_tile = lax.broadcasted_iota(jnp.int32, (heads, HEAD_SIZE), 1)
    marks = jnp.zeros((heads, HEAD_SIZE), jnp.float32)
    first_half = reqs // 2

    def part_sends(phase, first, count):
        return sends(
            phase,
            lambda k: part_send.at[peer(k), pl.ds(first, count)],
            lambda k: part_recv.at[k, pl.ds(first, count)],
        )

    for r in range(reqs):
        cache_copy[r].wait()
        limit = length_ref[0, r] - me * (span // groups)
        query_r = grouped[:, r * heads : (r + 1) * heads, :].reshape(n * heads, HEAD_SIZE)
        query_r = query_r.astype(jnp.bfloat16)
        top = jnp.full((heads, HEAD_SIZE), neutral, jnp.float32)
        for c in range(pieces):
            dots = lax.dot_general(
                query_r,
                cache[r, c * piece : (c + 1) * piece, :HEAD_SIZE],
                (((1,), (1,)), ((), ())),
                preferred_element_type=jnp.float32,
            )
            scores = dots[:heads]
            for g in range(1, groups):
                scores = jnp.where(
                    lane % groups == g, dots[g * heads : (g + 1) * heads], scores
                )
            usable = (lane + c * piece) // groups < limit
            scores = jnp.where(usable, scores * factor, neutral)
            score_ref[:, c * piece : (c + 1) * piece] = scores
            for i in range(piece // HEAD_SIZE):
                top = jnp.maximum(top, scores[:, i * HEAD_SIZE : (i + 1) * HEAD_SIZE])
        shift = groups
        while shift < HEAD_SIZE:
            top = jnp.maximum(top, pltpu.roll(top, shift, 1))
            shift *= 2
        top_wide = jnp.concatenate([top] * (piece // HEAD_SIZE), axis=1)
        total = jnp.zeros((heads, HEAD_SIZE), jnp.float32)
        acc = jnp.zeros((n * heads, HEAD_SIZE), jnp.float32)
        for c in range(pieces):
            usable = (lane + c * piece) // groups < limit
            weights = jnp.where(
                usable, jnp.exp(score_ref[:, c * piece : (c + 1) * piece] - top_wide), 0.0
            )
            for i in range(piece // HEAD_SIZE):
                total = total + weights[:, i * HEAD_SIZE : (i + 1) * HEAD_SIZE]
            spread = jnp.concatenate(
                [jnp.where(lane % groups == g, weights, 0.0) for g in range(groups)], axis=0
            ).astype(jnp.bfloat16)
            acc = acc + jnp.dot(
                spread,
                cache[r, c * piece : (c + 1) * piece, HEAD_SIZE:],
                preferred_element_type=jnp.float32,
            )
        shift = groups
        while shift < HEAD_SIZE:
            total = total + pltpu.roll(total, shift, 1)
            shift *= 2
        marks = jnp.where(lane_tile // groups == r, top, marks)
        marks = jnp.where(lane_tile // groups == reqs + r, total, marks)
        for g in range(groups):
            part_send[g, r] = acc[g * heads : (g + 1) * heads]
        if r == first_half - 1:
            early_copy = part_sends(2, 0, first_half)
            for copy in early_copy:
                copy.start()
    for g in range(groups):
        part_send[g, reqs] = marks
    part_copy = part_sends(4, first_half, reqs + 1 - first_half)
    for copy in part_copy:
        copy.start()
    part_copy = early_copy + part_copy
    part_recv[0] = part_send[me]
    for copy in part_copy:
        copy.wait_recv()

    tiles = [part_recv[k, reqs] for k in range(n)]
    highest = functools.reduce(jnp.maximum, tiles)
    scales = [jnp.exp(tile - highest) for tile in tiles]
    totals = sum(
        scale * pltpu.roll(tile, HEAD_SIZE - reqs * groups, 1)
        for scale, tile in zip(scales, tiles)
    )
    for r in range(reqs):
        chosen = lane_tile == r * groups + me

        def pick(tile):
            return jnp.sum(jnp.where(chosen, tile, 0.0), axis=1, keepdims=True)

        merged = sum(pick(scales[k]) * part_recv[k, r] for k in range(n))
        merged_top = pick(highest)
        top_all = jnp.maximum(merged_top, own_scores[r])
        old = jnp.exp(merged_top - top_all)
        new = jnp.exp(own_scores[r] - top_all)
        attended = (merged * old + new * value_ref[r : r + 1, :]) / (pick(totals) * old + new)
        for h in range(heads):
            flat_ref[r : r + 1, h * HEAD_SIZE : (h + 1) * HEAD_SIZE] = attended[h : h + 1]
    attended = flat_ref[...].astype(jnp.bfloat16)

    for copy in wo_copy:
        copy.wait()
    share_copy = sends(3, lambda k: share_send.at[peer(k)], lambda k: share_recv.at[k])
    for k in range(1, n):
        share_send[peer(k)] = jnp.dot(
            attended, wo[peer(k)], preferred_element_type=jnp.float32
        )
        share_copy[k - 1].start()
    mixed = jnp.dot(attended, wo[me], preferred_element_type=jnp.float32)
    for k in range(1, n):
        share_copy[k - 1].wait_recv()
        mixed = mixed + share_recv[k]
    out_ref[...] = mixed
    for copy in term_copy + query_copy + part_copy + share_copy:
        copy.wait_send()


def on_device_fused(
    tokens,
    gain,
    query_matrix,
    key_value_weight,
    output_weight,
    adapter_down_factors,
    adapter_up_query,
    adapter_up_key_value,
    tenant_slot_table,
    request_tenant_index,
    lengths,
    cache,
):
    n = lax.axis_size("tp")
    reqs, width = tokens.shape
    cols = query_matrix.shape[1]
    heads = cols // HEAD_SIZE
    rows = -(-(reqs * heads + reqs) // 8) * 8
    half = HEAD_SIZE // 2
    power = np.arange(HEAD_SIZE) % half * 2.0 / HEAD_SIZE
    frequency = jnp.asarray((theta_base ** -power).astype(np.float32)[None, :])
    smem = pl.BlockSpec(memory_space=pltpu.SMEM)
    vmem = pl.BlockSpec(memory_space=pltpu.VMEM)
    hbm = pl.BlockSpec(memory_space=pl.ANY)
    bf16, f32 = jnp.bfloat16, jnp.float32
    dma = pltpu.SemaphoreType.DMA
    share = pl.pallas_call(
        functools.partial(attention_kernel, n),
        out_shape=jax.ShapeDtypeStruct((reqs, cols), f32),
        in_specs=[smem] * 3 + [vmem] * 3 + [hbm] * 7,
        out_specs=vmem,
        scratch_shapes=[
            pltpu.VMEM((n, width // n, cols), bf16),
            pltpu.VMEM(key_value_weight.shape, bf16),
            pltpu.VMEM((n, output_weight.shape[0], width // n), bf16),
            pltpu.VMEM(cache.shape, bf16),
            pltpu.VMEM((6 * ADAPTER_RANK, width), bf16),
            pltpu.VMEM((2 * ADAPTER_RANK, adapter_up_query.shape[2]), bf16),
            pltpu.VMEM((2, 2 * ADAPTER_RANK, adapter_up_key_value.shape[3]), bf16),
            pltpu.VMEM((n, reqs, width // n), bf16),
            pltpu.VMEM((rows, HEAD_SIZE), f32),
            pltpu.VMEM((rows, HEAD_SIZE), f32),
            pltpu.VMEM((rows, HEAD_SIZE), f32),
            pltpu.VMEM((reqs, HEAD_SIZE), f32),
            pltpu.VMEM((n, reqs, cols + 2 * HEAD_SIZE), f32),
            pltpu.VMEM((n, reqs, cols + 2 * HEAD_SIZE), f32),
            pltpu.VMEM((n, reqs * heads, HEAD_SIZE), bf16),
            pltpu.VMEM((heads, cache.shape[1]), f32),
            pltpu.VMEM((n, reqs + 1, heads, HEAD_SIZE), f32),
            pltpu.VMEM((n, reqs + 1, heads, HEAD_SIZE), f32),
            pltpu.VMEM((reqs, cols), f32),
            pltpu.VMEM((n, reqs, width // n), f32),
            pltpu.VMEM((n, reqs, width // n), f32),
            dma((n,)),
            dma,
            dma((n,)),
            dma((reqs,)),
            dma((3,)),
            dma((3,)),
            dma((3,)),
            dma((5, n)),
            dma((5, n)),
        ],
        compiler_params=pltpu.CompilerParams(
            collective_id=0, has_side_effects=True, vmem_limit_bytes=60 * 2**20
        ),
    )(
        tenant_slot_table,
        request_tenant_index,
        lengths,
        tokens,
        gain,
        frequency,
        query_matrix,
        key_value_weight,
        output_weight,
        adapter_down_factors,
        adapter_up_query,
        adapter_up_key_value,
        cache,
    )
    return share.astype(bf16)


def solution(mesh):
    in_specs = (
        P(("rep", "dp"), None),
        P(),
        P(None, "tp"),
        P("tp", None),
        P("tp", None),
        P(("dp", "tp"), None, None),
        P(("dp", "tp"), None, None),
        P(("dp", "tp"), None, None, None),
        P(),
        P("rep"),
        P(("rep", "dp"), None),
        P(("rep", "dp"), "tp", None),
    )
    out_specs = P(("rep", "dp"), "tp")
    fused = mesh.shape["tp"] == KEY_VALUE_HEADS and mesh.shape["dp"] == 2
    body = on_device_fused if fused else on_device
    return jax.shard_map(
        body, mesh=mesh, in_specs=in_specs, out_specs=out_specs, check_vma=False
    )
```
